128 devices in a mesh: tm: 16 (over z_hi, y, core), pitch: 4 (over x), span: 2 (over z_lo).
Axes of the slice: x: 4, y: 4, z: 4 (z_hi: 2, z_lo: 2; z = z_hi * 2 + z_lo), core: 2. Of those that a mesh axis runs over, the one named last changes fastest.
Arguments:
- adjoint: float32 [16, 5, 64, 16, 256], P('tm', None, 'pitch', 'span'), may hold values from -6 to 6
- source: float32 [16, 5, 64, 16, 256], P('tm', None, 'pitch', 'span'), may hold values from -6 to 6
- face_jacobian: float32 [16, 3, 5, 5, 64, 16, 256], P('tm', None, None, None, 'pitch', 'span'), may hold values from -2 to 2
- dissipation: float32 [16, 3, 64, 16, 256], P('tm', None, 'pitch', 'span'), may hold values from 0.5 to 1.5
- cell_jacobian: float32 [16, 5, 5, 64, 16, 256], P('tm', None, None, 'pitch', 'span'), may hold values from -2 to 2
- pseudo_step: float32 [16, 64, 16, 256], P('tm', 'pitch', 'span'), may hold values from 0.02 to 0.1
Outputs:
- adjoint_next: float32 [16, 5, 64, 16, 256], P('tm', None, 'pitch', 'span')
- pseudo_residual: float32 [16, 5, 64, 16, 256], P('tm', None, 'pitch', 'span')
The draws below stay inside these ranges and needn't reach their ends.
All inputs are finite; a program needn't handle non-finite values.
Results may differ from the reference program's by a relative error of at most 0.0001.
Values sent between devices are 32-bit elements; how exact they have to be, the bound alone decides.
A program may use at most 128 MiB of HBM per device.

```python
import math
import jax
import jax.numpy as jnp
from jax import lax

FIELDS = 5
TIMES = 16
NP = 64
NR = 16
NA = 256


def block_scale(stream_key, dims, split, low, top_value):
    factor_of, own = 1.0, jax.random.fold_in(stream_key, 6)
    for dim, blocks in split:
        steps = jnp.exp(jax.random.uniform(jax.random.fold_in(own, dim), (blocks,), jnp.float32, low / len(split), top_value / len(split)))
        factor_of = factor_of * jnp.repeat(steps, dims[dim] // blocks).reshape([-1 if axis == dim else 1 for axis in range(len(dims))])
    return factor_of


def gaussian(own_key, shape, deviation, bound, cuts=(), kind=jnp.bfloat16):
    array = jax.random.normal(own_key, shape, jnp.float32) * deviation
    if len(cuts) > 0:
        array = block_scale(own_key, shape, cuts, -0.22, 0.18) * array
    return jnp.clip(array, min=-bound, max=bound).astype(kind)


def setup_inputs(seed: int = 0) -> dict:
    arg_keys = jax.random.split(jax.random.key(seed), 7)
    adjoint = gaussian(arg_keys[0], (TIMES, FIELDS, NP, NR, NA), 1.0, 6.0, ((0, 16), (2, 4), (3, 2)), jnp.float32)
    source = gaussian(arg_keys[1], (TIMES, FIELDS, NP, NR, NA), 1.0, 6.0, ((0, 16), (2, 4), (3, 2)), jnp.float32)
    face_jacobian = gaussian(arg_keys[2], (TIMES, 3, FIELDS, FIELDS, NP, NR, NA), 0.3, 2.0, ((0, 16), (4, 4), (5, 2)), jnp.float32)
    dissipation = jnp.clip(0.5 + 1.0 * jax.random.uniform(arg_keys[3], (TIMES, 3, NP, NR, NA), jnp.float32) ** block_scale(arg_keys[3], (TIMES, 3, NP, NR, NA), ((0, 16), (2, 4), (3, 2)), -0.2, 0.2), 0.5, 1.5)
    cell_jacobian = gaussian(arg_keys[4], (TIMES, FIELDS, FIELDS, NP, NR, NA), 0.3, 2.0, ((0, 16), (3, 4), (4, 2)), jnp.float32)
    pseudo_step = jnp.clip(jnp.exp(math.log(0.1) - 1.609438 * jax.random.uniform(arg_keys[5], (TIMES, NP, NR, NA), jnp.float32) ** block_scale(arg_keys[5], (TIMES, NP, NR, NA), ((0, 16), (1, 4), (2, 2)), -0.2, 0.2)), 0.02, 0.1)
    return dict(adjoint=adjoint, source=source, face_jacobian=face_jacobian, dissipation=dissipation, cell_jacobian=cell_jacobian, pseudo_step=pseudo_step)


frequency = 0.5
viscosity = 0.2
section_weights = (0.6, 0.6, 1.0)


def spectral_table(row_index, col_index, total):
    offset = (row_index[:, None] - col_index[None, :]) % total
    angle = math.pi * jnp.where(offset == 0, 1, offset).astype(jnp.float32) / total
    parity = (1 - 2 * (offset % 2)).astype(jnp.float32)
    sine = jnp.sin(angle)
    cosine = jnp.cos(angle)
    off_diag = parity * (frequency * 0.5 * cosine / sine + viscosity * 0.5 / (sine * sine))
    on_diag = viscosity * (total * total / 12.0 + 1.0 / 6.0)
    return jnp.where(offset == 0, jnp.float32(on_diag), off_diag).astype(jnp.float32)


def face_terms(jac_dir, dissip_dir, difference):
    turned = jnp.einsum('tbaprx,tbprx->taprx', jac_dir, difference, precision=lax.Precision.HIGHEST)
    spread = dissip_dir[:, None] * difference
    return 0.5 * (turned + spread), 0.5 * (turned - spread)


def residual_of(field, source, face_jacobian, dissipation, cell_jacobian, table):
    summed = jnp.zeros_like(field)
    for direction in range(3):
        axis_pos = 2 + direction
        length = field.shape[axis_pos]
        neighbor = jnp.roll(field, -1, axis_pos)
        difference = field - neighbor
        if direction > 0:
            shape_mask = [1, 1, 1, 1, 1]
            shape_mask[axis_pos] = length
            validity = (jnp.arange(length) < length - 1).astype(jnp.float32).reshape(shape_mask)
            difference = difference * validity
        forward_part, backward_part = face_terms(face_jacobian[:, direction], dissipation[:, direction], difference)
        summed = summed + forward_part + jnp.roll(backward_part, 1, axis_pos)
    summed = summed + jnp.einsum('tbaprx,tbprx->taprx', cell_jacobian, field, precision=lax.Precision.HIGHEST)
    summed = summed + jnp.einsum('mn,mfprx->nfprx', table, field, precision=lax.Precision.HIGHEST)
    return summed - source


def reference(adjoint, source, face_jacobian, dissipation, cell_jacobian, pseudo_step):
    total = adjoint.shape[0]
    index_all = jnp.arange(total, dtype=jnp.int32)
    table = spectral_table(index_all, index_all, total)
    first = residual_of(adjoint, source, face_jacobian, dissipation, cell_jacobian, table)
    current = adjoint - section_weights[0] * pseudo_step[:, None] * first
    for factor in section_weights[1:]:
        update = residual_of(current, source, face_jacobian, dissipation, cell_jacobian, table)
        current = adjoint - factor * pseudo_step[:, None] * update
    return current, first
```

```python
import functools
import math

import jax
import jax.numpy as jnp
import numpy as np
from jax import lax
from jax.experimental import pallas as pl
from jax.experimental.pallas import tpu as pltpu
from jax.sharding import PartitionSpec as P

MESH = pl.DeviceIdType.MESH
FREQUENCY = 0.5
VISCOSITY = 0.2
WEIGHTS = (0.6, 0.6, 1.0)
FIELDS, TIMES, LAYERS, ROWS, LANES, HALVES = 5, 16, 16, 8, 128, 2
GROUPS = LAYERS // ROWS


def spectral_table():
    k = (np.arange(TIMES)[:, None] - np.arange(TIMES)[None, :]) % TIMES
    angle = np.pi * np.where(k == 0, 1, k) / TIMES
    off = 0.5 * (-1.0) ** k * (FREQUENCY * np.cos(angle) / np.sin(angle) + VISCOSITY / np.sin(angle) ** 2)
    return np.where(k == 0, VISCOSITY * (TIMES * TIMES / 12.0 + 1.0 / 6.0), off)


def coupled(values):
    table = spectral_table()
    half = TIMES // 2
    even = 0.5 * (table[:half, :half] + table[half:, :half])
    odd = 0.5 * (table[:half, :half] - table[half:, :half])
    sums = [values[m] + values[m + half] for m in range(half)]
    diffs = [values[m] - values[m + half] for m in range(half)]
    low, high = [], []
    for n in range(half):
        e = sums[0] * np.float32(even[0, n])
        o = diffs[0] * np.float32(odd[0, n])
        for m in range(1, half):
            e = e + sums[m] * np.float32(even[m, n])
            o = o + diffs[m] * np.float32(odd[m, n])
        low.append(e + o)
        high.append(e - o)
    return low + high


def kernel(
    adj_hbm, src_hbm, fj_hbm, ds_hbm, cj_hbm, ps_hbm,
    next_ref, res_ref,
    adj, cur, acc, inb, osrc, outb, fj, cj, ds, ps, src,
    lps, lpb, hss, hsb, lss, lsb,
    load_sem, in_send, in_recv, out_send, out_recv, halo_send, halo_recv,
):
    tm, pitch, span = lax.axis_index("tm"), lax.axis_index("pitch"), lax.axis_index("span")
    pitches = lax.axis_size("pitch")
    other = 1 - span
    up, down = lax.rem(pitch + 1, pitches), lax.rem(pitch + pitches - 1, pitches)
    zh, y, core = tm // 8, lax.rem(tm // 2, 4), lax.rem(tm, 2)

    def target(k):
        q, j = k // 4, k % 4
        dz, dy, dc = (j // 2 + q // 2) % 2, (2 + 3 * j) % 4, q % 2
        return (lax.rem(zh + dz, 2) * 4 + lax.rem(y + dy, 4)) * 2 + lax.rem(core + dc, 2)

    targets = [target(k) for k in range(TIMES)]
    row = lax.broadcasted_iota(jnp.int32, (ROWS, LANES), 0)
    lane = lax.broadcasted_iota(jnp.int32, (ROWS, LANES), 1)

    def cols(h):
        return slice(h * LANES, (h + 1) * LANES)

    def wait_for(ref, sem):
        pltpu.make_async_copy(ref, ref, sem).wait()

    for h in range(HALVES):
        for f in range(FIELDS):
            pltpu.make_async_copy(
                adj_hbm.at[0, f, :, :, cols(h)], adj.at[h, pl.ds(0, LAYERS), f], load_sem.at[0]
            ).start()
    loads = [
        pltpu.make_async_copy(a.at[0], b, load_sem.at[1 + i])
        for i, (a, b) in enumerate(
            ((src_hbm, src), (cj_hbm, cj), (fj_hbm, fj), (ds_hbm, ds), (ps_hbm, ps))
        )
    ]
    for copy in loads:
        copy.start()
    zero = jnp.zeros((ROWS, LANES), jnp.float32)
    for h in range(HALVES):
        for f in range(FIELDS):
            for g in range(GROUPS):
                hsb[h, f, g] = zero
                lsb[h, f, g] = zero

    barrier = pltpu.get_barrier_semaphore()
    for w in targets:
        pl.semaphore_signal(barrier, inc=1, device_id=(w, pitch, other), device_id_type=MESH)
    for p in (down, up):
        pl.semaphore_signal(barrier, inc=1, device_id=(tm, p, span), device_id_type=MESH)
    pl.semaphore_wait(barrier, TIMES + 2)
    wait_for(adj.at[:, pl.ds(0, LAYERS)], load_sem.at[0])

    def send_in(field, h, w):
        pltpu.make_async_remote_copy(
            src_ref=field.at[h, w], dst_ref=inb.at[h, tm],
            send_sem=in_send.at[h], recv_sem=in_recv.at[h],
            device_id=(w, pitch, other), device_id_type=MESH,
        ).start()

    def send_out(h, w):
        pltpu.make_async_remote_copy(
            src_ref=osrc.at[h, w], dst_ref=outb.at[h, tm],
            send_sem=out_send.at[h], recv_sem=out_recv.at[h],
            device_id=(w, pitch, other), device_id_type=MESH,
        ).start()

    def halo(i, source, dest, device):
        return pltpu.make_async_remote_copy(
            src_ref=source, dst_ref=dest, send_sem=halo_send.at[i], recv_sem=halo_recv.at[i],
            device_id=device, device_id_type=MESH,
        )

    def pack_first_rows(field):
        def body(g, c):
            for h in range(HALVES):
                for f in range(FIELDS):
                    tile = field[h, g * ROWS, f]
                    for j in range(1, ROWS):
                        tile = jnp.where(row == j, pltpu.roll(field[h, g * ROWS + j, f], j, 0), tile)
                    hss[h, f, g] = tile
            return c
        lax.fori_loop(0, GROUPS, body, 0)

    def face(d, l, h, diff):
        turned = []
        for a in range(FIELDS):
            s = fj[d, 0, a, l, :, cols(h)] * diff[0]
            for b in range(1, FIELDS):
                s = s + fj[d, b, a, l, :, cols(h)] * diff[b]
            turned.append(s)
        spread = [ds[d, l, :, cols(h)] * x for x in diff]
        return [t + s for t, s in zip(turned, spread)], [t - s for t, s in zip(turned, spread)]

    def pitch_face(field, l, h):
        diff = [0.5 * (field[h, l, f] - field[h, l + 1, f]) for f in range(FIELDS)]
        return face(0, l, h, diff)

    def near_layer(field, l, below, with_pitch):
        lows = []
        v = [[field[h, l, f] for f in range(FIELDS)] for h in range(HALVES)]
        carried = None
        for h in range(HALVES):
            total = [below[h * FIELDS + f] - src[f, l, :, cols(h)] for f in range(FIELDS)]
            for a in range(FIELDS):
                for b in range(FIELDS):
                    total[a] = total[a] + cj[b, a, l, :, cols(h)] * v[h][b]
            if with_pitch:
                upper, lower = pitch_face(field, l, h)
                total = [t + u for t, u in zip(total, upper)]
                lows += lower
            diff = []
            for f in range(FIELDS):
                after = pltpu.roll(v[h][f], LANES - 1, 1)
                if h + 1 < HALVES:
                    after = jnp.where(lane == LANES - 1, pltpu.roll(v[h + 1][f], LANES - 1, 1), after)
                    diff.append(0.5 * (v[h][f] - after))
                else:
                    diff.append(jnp.where(lane == LANES - 1, 0.0, 0.5 * (v[h][f] - after)))
            upper, lower = face(2, l, h, diff)
            turned = [pltpu.roll(x, 1, 1) for x in lower]
            for f in range(FIELDS):
                first = 0.0 if carried is None else carried[f]
                total[f] = total[f] + upper[f] + jnp.where(lane == 0, first, turned[f])
                acc[h, l, f] = total[f]
            carried = turned
        return lows

    def near(field):
        def body(l, below):
            return tuple(near_layer(field, l, below, True))
        below = lax.fori_loop(0, LAYERS - 1, body, (zero,) * (HALVES * FIELDS))
        near_layer(field, LAYERS - 1, below, False)

    def far(field):
        for h in range(HALVES):
            upper, lower = pitch_face(field, LAYERS - 1, h)
            for f in range(FIELDS):
                acc[h, LAYERS - 1, f] += upper[f]
                lps[h, f] = lower[f]
        halo(1, lps, lpb, (tm, up, span)).start()

        def body(g, c):
            for h in range(HALVES):
                packed = [zero] * FIELDS
                above = [hsb[h, f, g] for f in range(FIELDS)]
                for j in range(ROWS):
                    l = g * ROWS + j
                    diff = []
                    for f in range(FIELDS):
                        v = field[h, l, f]
                        edge = pltpu.roll(above[f], ROWS - 1 - j, 0) if j < ROWS - 1 else above[f]
                        after = jnp.where(row == ROWS - 1, edge, pltpu.roll(v, ROWS - 1, 0))
                        missing = (row == ROWS - 1) & (span == 1)
                        diff.append(jnp.where(missing, 0.0, 0.5 * (v - after)))
                    upper, lower = face(1, l, h, diff)
                    for f in range(FIELDS):
                        turned = pltpu.roll(lower[f], 1, 0)
                        acc[h, l, f] += upper[f] + jnp.where(row == 0, 0.0, turned)
                        moved = pltpu.roll(turned, j, 0) if j else turned
                        packed[f] = jnp.where(row == j, moved, packed[f])
                for f in range(FIELDS):
                    lss[h, f, g] = packed[f]
            return c
        lax.fori_loop(0, GROUPS, body, 0)

    def finish_acc():
        for h in range(HALVES):
            for f in range(FIELDS):
                acc[h, 0, f] += lpb[h, f]

        def body(g, c):
            for h in range(HALVES):
                for f in range(FIELDS):
                    below = lsb[h, f, g]
                    for j in range(ROWS):
                        moved = pltpu.roll(below, ROWS - j, 0) if j else below
                        acc[h, g * ROWS + j, f] += jnp.where(row == 0, moved, 0.0)
            return c
        lax.fori_loop(0, GROUPS, body, 0)

    def couple(h):
        def body(f, c):
            out = coupled([inb[h, m, f] for m in range(TIMES)])
            for n in range(TIMES):
                osrc[h, n, f] = out[n]
            return c
        lax.fori_loop(0, FIELDS, body, 0)
        for w in targets:
            send_out(h, w)

    for step, weight in enumerate(WEIGHTS):
        first, last = step == 0, step == len(WEIGHTS) - 1
        field = adj if first else cur
        if first:
            for w in targets:
                send_in(field, 0, w)
        halo(0, field.at[:, 0], field.at[:, LAYERS], (tm, down, span)).start()
        pack_first_rows(field)

        @pl.when(span == 1)
        def _():
            halo(2, hss, hsb, (tm, pitch, other)).start()

        if first:
            for w in targets:
                send_in(field, 1, w)
            for copy in loads:
                copy.wait()
        near(field)

        wait_for(inb.at[0], in_recv.at[0])
        couple(0)

        wait_for(field.at[:, LAYERS], halo_recv.at[0])

        @pl.when(span == 0)
        def _():
            wait_for(hsb, halo_recv.at[2])

        far(field)

        @pl.when(span == 0)
        def _():
            halo(3, lss, lsb, (tm, pitch, other)).start()

        wait_for(inb.at[1], in_recv.at[1])
        couple(1)

        wait_for(lpb, halo_recv.at[1])

        @pl.when(span == 1)
        def _():
            wait_for(lsb, halo_recv.at[3])

        finish_acc()

        wait_for(field.at[:, 0], halo_send.at[0])
        wait_for(lps, halo_send.at[1])

        @pl.when(span == 1)
        def _():
            wait_for(hss, halo_send.at[2])

        @pl.when(span == 0)
        def _():
            wait_for(lss, halo_send.at[3])

        for h in range(HALVES):
            wait_for(field.at[h, pl.ds(0, LAYERS)], in_send.at[h])
            wait_for(outb.at[h], out_recv.at[h])
            for w in targets:
                pace = ps[w, :, cols(h)] * np.float32(weight)
                for f in range(FIELDS):
                    residual = acc[h, w, f] + outb[h, w, f]
                    if first:
                        res_ref[0, f, w, :, cols(h)] = residual
                    new = adj[h, w, f] - pace * residual
                    if last:
                        next_ref[0, f, w, :, cols(h)] = new
                    else:
                        cur[h, w, f] = new
                if not last:
                    send_in(cur, h, w)
            wait_for(osrc.at[h], out_send.at[h])


def local(adjoint, source, face_jacobian, dissipation, cell_jacobian, pseudo_step):
    f32 = jnp.float32
    tile = (ROWS, LANES)
    block = (HALVES, LAYERS, FIELDS) + tile
    tall = (HALVES, LAYERS + 1, FIELDS) + tile
    edge = (HALVES, FIELDS) + tile
    rows = (HALVES, FIELDS, GROUPS) + tile
    vmem = [
        tall, tall, block, block, block, block,
        face_jacobian.shape[1:], cell_jacobian.shape[1:], dissipation.shape[1:],
        pseudo_step.shape[1:], source.shape[1:],
        edge, edge, rows, rows, rows, rows,
    ]
    dma = pltpu.SemaphoreType.DMA
    out = jax.ShapeDtypeStruct(adjoint.shape, f32)
    return pl.pallas_call(
        kernel,
        out_shape=(out, out),
        in_specs=[pl.BlockSpec(memory_space=pl.ANY)] * 6,
        out_specs=(pl.BlockSpec(memory_space=pltpu.VMEM),) * 2,
        scratch_shapes=[pltpu.VMEM(s, f32) for s in vmem]
        + [dma((6,)), dma((2,)), dma((2,)), dma((2,)), dma((2,)), dma((4,)), dma((4,))],
        compiler_params=pltpu.CompilerParams(
            collective_id=0, has_side_effects=True, vmem_limit_bytes=48 * 2**20
        ),
        name="adjoint_update",
    )(adjoint, source, face_jacobian, dissipation, cell_jacobian, pseudo_step)


def solution(mesh):
    in_specs = (
        P("tm", None, "pitch", "span", None),
        P("tm", None, "pitch", "span", None),
        P("tm", None, None, None, "pitch", "span", None),
        P("tm", None, "pitch", "span", None),
        P("tm", None, None, "pitch", "span", None),
        P("tm", "pitch", "span", None),
    )
    out_specs = (P("tm", None, "pitch", "span", None), P("tm", None, "pitch", "span", None))
    return jax.shard_map(local, mesh=mesh, in_specs=in_specs, out_specs=out_specs, check_vma=False)
```

```python
import functools
import math

import jax
import jax.numpy as jnp
import numpy as np
from jax import lax
from jax.experimental import pallas as pl
from jax.experimental.pallas import tpu as pltpu
from jax.sharding import PartitionSpec as P

MESH = pl.DeviceIdType.MESH
FREQUENCY = 0.5
VISCOSITY = 0.2
WEIGHTS = (0.6, 0.6, 1.0)
FIELDS, TIMES, LAYERS, ROWS, LANES, HALVES = 5, 16, 16, 8, 128, 2
GROUPS = LAYERS // ROWS


def spectral_table():
    k = (np.arange(TIMES)[:, None] - np.arange(TIMES)[None, :]) % TIMES
    angle = np.pi * np.where(k == 0, 1, k) / TIMES
    off = 0.5 * (-1.0) ** k * (FREQUENCY * np.cos(angle) / np.sin(angle) + VISCOSITY / np.sin(angle) ** 2)
    return np.where(k == 0, VISCOSITY * (TIMES * TIMES / 12.0 + 1.0 / 6.0), off)


def coupled(values):
    table = spectral_table()
    half = TIMES // 2
    even = 0.5 * (table[:half, :half] + table[half:, :half])
    odd = 0.5 * (table[:half, :half] - table[half:, :half])
    sums = [values[m] + values[m + half] for m in range(half)]
    diffs = [values[m] - values[m + half] for m in range(half)]
    low, high = [], []
    for n in range(half):
        e = sums[0] * np.float32(even[0, n])
        o = diffs[0] * np.float32(odd[0, n])
        for m in range(1, half):
            e = e + sums[m] * np.float32(even[m, n])
            o = o + diffs[m] * np.float32(odd[m, n])
        low.append(e + o)
        high.append(e - o)
    return low + high


def kernel(
    adj_hbm, src_hbm, fj_hbm, ds_hbm, cj_hbm, ps_hbm,
    next_ref, res_ref,
    adj, cur, acc, inb, osrc, outb, fj, cj, ds, ps, src,
    lps, lpb, hss, hsb, lss, lsb,
    load_sem, in_send, in_recv, out_send, out_recv, halo_send, halo_recv,
):
    tm, pitch, span = lax.axis_index("tm"), lax.axis_index("pitch"), lax.axis_index("span")
    pitches = lax.axis_size("pitch")
    other = 1 - span
    up, down = lax.rem(pitch + 1, pitches), lax.rem(pitch + pitches - 1, pitches)
    zh, y, core = tm // 8, lax.rem(tm // 2, 4), lax.rem(tm, 2)

    def target(k):
        q, j = k // 4, k % 4
        dz, dy, dc = (j // 2 + q // 2) % 2, (2 + 3 * j) % 4, q % 2
        return (lax.rem(zh + dz, 2) * 4 + lax.rem(y + dy, 4)) * 2 + lax.rem(core + dc, 2)

    targets = [target(k) for k in range(TIMES)]
    row = lax.broadcasted_iota(jnp.int32, (ROWS, LANES), 0)
    lane = lax.broadcasted_iota(jnp.int32, (ROWS, LANES), 1)

    def cols(h):
        return slice(h * LANES, (h + 1) * LANES)

    def wait_for(ref, sem):
        pltpu.make_async_copy(ref, ref, sem).wait()

    for h in range(HALVES):
        for f in range(FIELDS):
            pltpu.make_async_copy(
                adj_hbm.at[0, f, :, :, cols(h)], adj.at[h, pl.ds(0, LAYERS), f], load_sem.at[0]
            ).start()
    loads = [
        pltpu.make_async_copy(a.at[0], b, load_sem.at[1 + i])
        for i, (a, b) in enumerate(
            ((src_hbm, src), (cj_hbm, cj), (fj_hbm, fj), (ds_hbm, ds), (ps_hbm, ps))
        )
    ]
    zero = jnp.zeros((ROWS, LANES), jnp.float32)
    for h in range(HALVES):
        for f in range(FIELDS):
            for g in range(GROUPS):
                hsb[h, f, g] = zero
                lsb[h, f, g] = zero

    def pack_first_rows(field, h):
        for f in range(FIELDS):
            for g in range(GROUPS):
                tile = field[h, g * ROWS, f]
                for j in range(1, ROWS):
                    tile = jnp.where(row == j, pltpu.roll(field[h, g * ROWS + j, f], j, 0), tile)
                hss[h, f, g] = tile

    barrier = pltpu.get_barrier_semaphore()
    for w in targets:
        pl.semaphore_signal(barrier, inc=1, device_id=(w, pitch, other), device_id_type=MESH)
    for p in (down, up):
        pl.semaphore_signal(barrier, inc=1, device_id=(tm, p, span), device_id_type=MESH)
    wait_for(adj.at[:, pl.ds(0, LAYERS)], load_sem.at[0])
    for copy in loads:
        copy.start()
    for h in range(HALVES):
        pack_first_rows(adj, h)
    pl.semaphore_wait(barrier, TIMES + 2)

    def send_in(field, h, w):
        pltpu.make_async_remote_copy(
            src_ref=field.at[h, w], dst_ref=inb.at[h, tm],
            send_sem=in_send.at[h], recv_sem=in_recv.at[h],
            device_id=(w, pitch, other), device_id_type=MESH,
        ).start()

    def send_out(h, w):
        pltpu.make_async_remote_copy(
            src_ref=osrc.at[h, w], dst_ref=outb.at[h, tm],
            send_sem=out_send.at[h], recv_sem=out_recv.at[h],
            device_id=(w, pitch, other), device_id_type=MESH,
        ).start()

    def halo(i, h, source, dest, device):
        return pltpu.make_async_remote_copy(
            src_ref=source, dst_ref=dest, send_sem=halo_send.at[i, h], recv_sem=halo_recv.at[i, h],
            device_id=device, device_id_type=MESH,
        )

    def rows_out(i, h, source, dest):
        halo(i, h, source.at[h], dest.at[h], (tm, pitch, other)).start()

    def send_field(field, h):
        @pl.when(span == 1)
        def _():
            rows_out(2, h, hss, hsb)

        halo(0, h, field.at[h, 0], field.at[h, LAYERS], (tm, down, span)).start()
        for w in targets:
            send_in(field, h, w)

    def sent_field(field, h):
        @pl.when(span == 1)
        def _():
            wait_for(hss.at[h], halo_send.at[2, h])

        wait_for(field.at[h, 0], halo_send.at[0, h])
        wait_for(field.at[h, pl.ds(0, LAYERS)], in_send.at[h])

    def face(d, l, h, diff):
        turned = []
        for a in range(FIELDS):
            s = fj[d, 0, a, l, :, cols(h)] * diff[0]
            for b in range(1, FIELDS):
                s = s + fj[d, b, a, l, :, cols(h)] * diff[b]
            turned.append(s)
        spread = [ds[d, l, :, cols(h)] * x for x in diff]
        return [t + s for t, s in zip(turned, spread)], [t - s for t, s in zip(turned, spread)]

    def pitch_face(field, l, h):
        diff = [0.5 * (field[h, l, f] - field[h, l + 1, f]) for f in range(FIELDS)]
        return face(0, l, h, diff)

    def near_layer(field, l, below, with_pitch):
        lows = []
        v = [[field[h, l, f] for f in range(FIELDS)] for h in range(HALVES)]
        carried = None
        for h in range(HALVES):
            total = [below[h * FIELDS + f] - src[f, l, :, cols(h)] for f in range(FIELDS)]
            for a in range(FIELDS):
                for b in range(FIELDS):
                    total[a] = total[a] + cj[b, a, l, :, cols(h)] * v[h][b]
            if with_pitch:
                upper, lower = pitch_face(field, l, h)
                total = [t + u for t, u in zip(total, upper)]
                lows += lower
            diff = []
            for f in range(FIELDS):
                after = pltpu.roll(v[h][f], LANES - 1, 1)
                if h + 1 < HALVES:
                    after = jnp.where(lane == LANES - 1, pltpu.roll(v[h + 1][f], LANES - 1, 1), after)
                    diff.append(0.5 * (v[h][f] - after))
                else:
                    diff.append(jnp.where(lane == LANES - 1, 0.0, 0.5 * (v[h][f] - after)))
            upper, lower = face(2, l, h, diff)
            turned = [pltpu.roll(x, 1, 1) for x in lower]
            for f in range(FIELDS):
                first = 0.0 if carried is None else carried[f]
                total[f] = total[f] + upper[f] + jnp.where(lane == 0, first, turned[f])
                acc[h, l, f] += total[f]
            carried = turned
        return lows

    def near(field):
        def body(l, below):
            return tuple(near_layer(field, l, below, True))
        below = lax.fori_loop(0, LAYERS - 1, body, (zero,) * (HALVES * FIELDS))
        near_layer(field, LAYERS - 1, below, False)

    def far(field, h):
        wait_for(field.at[h, LAYERS], halo_recv.at[0, h])
        last_upper, lower = pitch_face(field, LAYERS - 1, h)
        for f in range(FIELDS):
            lps[h, f] = lower[f]
        halo(1, h, lps.at[h], lpb.at[h], (tm, up, span)).start()

        @pl.when(span == 0)
        def _():
            wait_for(hsb.at[h], halo_recv.at[2, h])

        def body(g, c):
            packed = [zero] * FIELDS
            above = [hsb[h, f, g] for f in range(FIELDS)]
            for j in range(ROWS):
                l = g * ROWS + j
                diff = []
                for f in range(FIELDS):
                    v = field[h, l, f]
                    edge = pltpu.roll(above[f], ROWS - 1 - j, 0) if j < ROWS - 1 else above[f]
                    after = jnp.where(row == ROWS - 1, edge, pltpu.roll(v, ROWS - 1, 0))
                    missing = (row == ROWS - 1) & (span == 1)
                    diff.append(jnp.where(missing, 0.0, 0.5 * (v - after)))
                upper, lower = face(1, l, h, diff)
                for f in range(FIELDS):
                    turned = pltpu.roll(lower[f], 1, 0)
                    acc[h, l, f] = upper[f] + jnp.where(row == 0, 0.0, turned)
                    moved = pltpu.roll(turned, j, 0) if j else turned
                    packed[f] = jnp.where(row == j, moved, packed[f])
            for f in range(FIELDS):
                lss[h, f, g] = packed[f]
            return c
        lax.fori_loop(0, GROUPS, body, 0)

        @pl.when(span == 0)
        def _():
            rows_out(3, h, lss, lsb)

        for f in range(FIELDS):
            acc[h, LAYERS - 1, f] += last_upper[f]

    def couple(h, first):
        def body(f, c):
            out = coupled([inb[h, m, f] for m in range(TIMES)])
            for n in range(TIMES):
                osrc[h, n, f] = out[n]
            return c
        if not first:
            wait_for(osrc.at[h], out_send.at[h])
        lax.fori_loop(0, FIELDS, body, 0)
        for w in targets:
            send_out(h, w)

    def update(field, h, weight, first, last):
        wait_for(lpb.at[h], halo_recv.at[1, h])

        @pl.when(span == 1)
        def _():
            wait_for(lsb.at[h], halo_recv.at[3, h])

        wait_for(outb.at[h], out_recv.at[h])
        sent_field(field, h)
        wait_for(lps.at[h], halo_send.at[1, h])

        @pl.when(span == 0)
        def _():
            wait_for(lss.at[h], halo_send.at[3, h])

        for g in range(GROUPS):
            below = [lsb[h, f, g] for f in range(FIELDS)]
            packed = [None] * FIELDS
            for j in range(ROWS):
                l = g * ROWS + j
                pace = ps[l, :, cols(h)] * np.float32(weight)
                for f in range(FIELDS):
                    moved = pltpu.roll(below[f], ROWS - j, 0) if j else below[f]
                    residual = acc[h, l, f] + outb[h, l, f] + jnp.where(row == 0, moved, 0.0)
                    if l == 0:
                        residual = residual + lpb[h, f]
                    if first:
                        res_ref[0, f, l, :, cols(h)] = residual
                    new = adj[h, l, f] - pace * residual
                    if last:
                        next_ref[0, f, l, :, cols(h)] = new
                    else:
                        cur[h, l, f] = new
                        packed[f] = jnp.where(row == j, pltpu.roll(new, j, 0), packed[f]) if j else new
            if not last:
                for f in range(FIELDS):
                    hss[h, f, g] = packed[f]
        if not last:
            send_field(cur, h)

    send_field(adj, 0)
    for copy in loads:
        copy.wait()
    send_field(adj, 1)

    for step, weight in enumerate(WEIGHTS):
        first, last = step == 0, step == len(WEIGHTS) - 1
        field = adj if first else cur
        wait_for(inb.at[0], in_recv.at[0])
        couple(0, first)
        for h in range(HALVES):
            far(field, h)
        near(field)
        wait_for(inb.at[1], in_recv.at[1])
        couple(1, first)
        for h in range(HALVES):
            update(field, h, weight, first, last)
    for h in range(HALVES):
        wait_for(osrc.at[h], out_send.at[h])


def local(adjoint, source, face_jacobian, dissipation, cell_jacobian, pseudo_step):
    f32 = jnp.float32
    tile = (ROWS, LANES)
    block = (HALVES, LAYERS, FIELDS) + tile
    tall = (HALVES, LAYERS + 1, FIELDS) + tile
    edge = (HALVES, FIELDS) + tile
    rows = (HALVES, FIELDS, GROUPS) + tile
    vmem = [
        tall, tall, block, block, block, block,
        face_jacobian.shape[1:], cell_jacobian.shape[1:], dissipation.shape[1:],
        pseudo_step.shape[1:], source.shape[1:],
        edge, edge, rows, rows, rows, rows,
    ]
    dma = pltpu.SemaphoreType.DMA
    out = jax.ShapeDtypeStruct(adjoint.shape, f32)
    return pl.pallas_call(
        kernel,
        out_shape=(out, out),
        in_specs=[pl.BlockSpec(memory_space=pl.ANY)] * 6,
        out_specs=(pl.BlockSpec(memory_space=pltpu.VMEM),) * 2,
        scratch_shapes=[pltpu.VMEM(s, f32) for s in vmem]
        + [dma((6,)), dma((2,)), dma((2,)), dma((2,)), dma((2,)), dma((4, 2)), dma((4, 2))],
        compiler_params=pltpu.CompilerParams(
            collective_id=0, has_side_effects=True, vmem_limit_bytes=48 * 2**20
        ),
        name="adjoint_update",
    )(*(
        pltpu.with_memory_space_constraint(x, pltpu.HBM)
        for x in (adjoint, source, face_jacobian, dissipation, cell_jacobian, pseudo_step)
    ))


def solution(mesh):
    in_specs = (
        P("tm", None, "pitch", "span", None),
        P("tm", None, "pitch", "span", None),
        P("tm", None, None, None, "pitch", "span", None),
        P("tm", None, "pitch", "span", None),
        P("tm", None, None, "pitch", "span", None),
        P("tm", "pitch", "span", None),
    )
    out_specs = (P("tm", None, "pitch", "span", None), P("tm", None, "pitch", "span", None))
    return jax.shard_map(local, mesh=mesh, in_specs=in_specs, out_specs=out_specs, check_vma=False)
```

```python
import functools
import math

import jax
import jax.numpy as jnp
import numpy as np
from jax import lax
from jax.experimental import pallas as pl
from jax.experimental.pallas import tpu as pltpu
from jax.sharding import PartitionSpec as P

MESH = pl.DeviceIdType.MESH
FREQUENCY = 0.5
VISCOSITY = 0.2
WEIGHTS = (0.6, 0.6, 1.0)
FIELDS, TIMES, LAYERS, ROWS, LANES, HALVES = 5, 16, 16, 8, 128, 2
GROUPS = LAYERS // ROWS
EARLY = 8
FIRST = ("S0", "P1", "L", "Q1", "F0", "C0", "N", "F1", "C1", "U0", "U1")
ORDER = ("F0", "C0", "N", "F1", "C1", "U0", "U1")


def spectral_table():
    k = (np.arange(TIMES)[:, None] - np.arange(TIMES)[None, :]) % TIMES
    angle = np.pi * np.where(k == 0, 1, k) / TIMES
    off = 0.5 * (-1.0) ** k * (FREQUENCY * np.cos(angle) / np.sin(angle) + VISCOSITY / np.sin(angle) ** 2)
    return np.where(k == 0, VISCOSITY * (TIMES * TIMES / 12.0 + 1.0 / 6.0), off)


def coupled(values):
    table = spectral_table()
    half = TIMES // 2
    even = 0.5 * (table[:half, :half] + table[half:, :half])
    odd = 0.5 * (table[:half, :half] - table[half:, :half])
    sums = [values[m] + values[m + half] for m in range(half)]
    diffs = [values[m] - values[m + half] for m in range(half)]
    low, high = [], []
    for n in range(half):
        e = sums[0] * np.float32(even[0, n])
        o = diffs[0] * np.float32(odd[0, n])
        for m in range(1, half):
            e = e + sums[m] * np.float32(even[m, n])
            o = o + diffs[m] * np.float32(odd[m, n])
        low.append(e + o)
        high.append(e - o)
    return low + high


def kernel(
    adj_hbm, src_hbm, fj_hbm, ds_hbm, cj_hbm, ps_hbm,
    next_ref, res_ref,
    adj, cur, acc, inb, osrc, outb, fj, cj, ds, ps, src,
    lps, lpb, hss, hsb, lss, lsb,
    load_sem, in_send, in_recv, out_send, out_recv, halo_send, halo_recv,
):
    tm, pitch, span = lax.axis_index("tm"), lax.axis_index("pitch"), lax.axis_index("span")
    pitches = lax.axis_size("pitch")
    other = 1 - span
    up, down = lax.rem(pitch + 1, pitches), lax.rem(pitch + pitches - 1, pitches)
    zh, y, core = tm // 8, lax.rem(tm // 2, 4), lax.rem(tm, 2)

    def target(k):
        q, j = k // 4, k % 4
        dz, dy, dc = (j // 2 + q // 2) % 2, (2 + 3 * j) % 4, q % 2
        return (lax.rem(zh + dz, 2) * 4 + lax.rem(y + dy, 4)) * 2 + lax.rem(core + dc, 2)

    targets = [target(k) for k in range(TIMES)]
    row = lax.broadcasted_iota(jnp.int32, (ROWS, LANES), 0)
    lane = lax.broadcasted_iota(jnp.int32, (ROWS, LANES), 1)

    def cols(h):
        return slice(h * LANES, (h + 1) * LANES)

    def wait_for(ref, sem):
        pltpu.make_async_copy(ref, ref, sem).wait()

    for h in range(HALVES):
        for f in range(FIELDS):
            pltpu.make_async_copy(
                adj_hbm.at[0, f, :, :, cols(h)], adj.at[h, pl.ds(0, LAYERS), f], load_sem.at[0]
            ).start()
    loads = [
        pltpu.make_async_copy(a.at[0], b, load_sem.at[1 + i])
        for i, (a, b) in enumerate(
            ((src_hbm, src), (cj_hbm, cj), (fj_hbm, fj), (ds_hbm, ds), (ps_hbm, ps))
        )
    ]
    zero = jnp.zeros((ROWS, LANES), jnp.float32)
    for h in range(HALVES):
        for f in range(FIELDS):
            for g in range(GROUPS):
                hsb[h, f, g] = zero
                lsb[h, f, g] = zero

    def pack_first_rows(field, h):
        for f in range(FIELDS):
            for g in range(GROUPS):
                tile = field[h, g * ROWS, f]
                for j in range(1, ROWS):
                    tile = jnp.where(row == j, pltpu.roll(field[h, g * ROWS + j, f], j, 0), tile)
                hss[h, f, g] = tile

    barrier = pltpu.get_barrier_semaphore()
    for w in targets:
        pl.semaphore_signal(barrier, inc=1, device_id=(w, pitch, other), device_id_type=MESH)
    for p in (down, up):
        pl.semaphore_signal(barrier, inc=1, device_id=(tm, p, span), device_id_type=MESH)
    wait_for(adj.at[:, pl.ds(0, LAYERS)], load_sem.at[0])
    for copy in loads:
        copy.start()
    for h in range(HALVES):
        pack_first_rows(adj, h)

    def clear(l, c):
        for h in range(HALVES):
            for f in range(FIELDS):
                acc[h, l, f] = zero
        return c
    lax.fori_loop(0, LAYERS, clear, 0)
    pl.semaphore_wait(barrier, TIMES + 2)

    def send_in(field, h, w):
        pltpu.make_async_remote_copy(
            src_ref=field.at[h, w], dst_ref=inb.at[h, tm],
            send_sem=in_send.at[h], recv_sem=in_recv.at[h],
            device_id=(w, pitch, other), device_id_type=MESH,
        ).start()

    def send_out(h, w):
        pltpu.make_async_remote_copy(
            src_ref=osrc.at[h, w], dst_ref=outb.at[h, tm],
            send_sem=out_send.at[h], recv_sem=out_recv.at[h],
            device_id=(w, pitch, other), device_id_type=MESH,
        ).start()

    def halo(i, h, source, dest, device):
        return pltpu.make_async_remote_copy(
            src_ref=source, dst_ref=dest, send_sem=halo_send.at[i, h], recv_sem=halo_recv.at[i, h],
            device_id=device, device_id_type=MESH,
        )

    def rows_out(i, h, source, dest):
        halo(i, h, source.at[h], dest.at[h], (tm, pitch, other)).start()

    def send_field(field, h, start=0, stop=TIMES):
        if start == 0:
            @pl.when(span == 1)
            def _():
                rows_out(2, h, hss, hsb)

            halo(0, h, field.at[h, 0], field.at[h, LAYERS], (tm, down, span)).start()
        for w in targets[start:stop]:
            send_in(field, h, w)

    def sent_field(field, h):
        @pl.when(span == 1)
        def _():
            wait_for(hss.at[h], halo_send.at[2, h])

        wait_for(field.at[h, 0], halo_send.at[0, h])
        wait_for(field.at[h, pl.ds(0, LAYERS)], in_send.at[h])

    def face(d, l, h, diff):
        turned = []
        for a in range(FIELDS):
            s = fj[d, 0, a, l, :, cols(h)] * diff[0]
            for b in range(1, FIELDS):
                s = s + fj[d, b, a, l, :, cols(h)] * diff[b]
            turned.append(s)
        spread = [ds[d, l, :, cols(h)] * x for x in diff]
        return [t + s for t, s in zip(turned, spread)], [t - s for t, s in zip(turned, spread)]

    def pitch_face(field, l, h):
        diff = [0.5 * (field[h, l, f] - field[h, l + 1, f]) for f in range(FIELDS)]
        return face(0, l, h, diff)

    def near(field):
        def body(l, c, with_pitch):
            carried = None
            for h in range(HALVES):
                v = [field[h, l, f] for f in range(FIELDS)]
                diff = []
                for f in range(FIELDS):
                    after = pltpu.roll(v[f], LANES - 1, 1)
                    if h + 1 < HALVES:
                        beyond = pltpu.roll(field[h + 1, l, f], LANES - 1, 1)
                        diff.append(0.5 * (v[f] - jnp.where(lane == LANES - 1, beyond, after)))
                    else:
                        diff.append(jnp.where(lane == LANES - 1, 0.0, 0.5 * (v[f] - after)))
                upper, lower = face(2, l, h, diff)
                turned = [pltpu.roll(x, 1, 1) for x in lower]
                for f in range(FIELDS):
                    first = 0.0 if carried is None else carried[f]
                    total = acc[h, l, f] - src[f, l, :, cols(h)] + upper[f]
                    for b in range(FIELDS):
                        total = total + cj[b, f, l, :, cols(h)] * v[b]
                    acc[h, l, f] = total + jnp.where(lane == 0, first, turned[f])
                carried = turned
                if with_pitch:
                    upper, lower = pitch_face(field, l, h)
                    for f in range(FIELDS):
                        acc[h, l, f] += upper[f]
                        acc[h, l + 1, f] += lower[f]
            return c
        def group(g, c):
            for j in range(4):
                body(g * 4 + j, 0, with_pitch=True)
            return c
        lax.fori_loop(0, LAYERS // 4 - 1, group, 0)
        for l in range(LAYERS - 4, LAYERS):
            body(l, 0, with_pitch=l < LAYERS - 1)

    def far(field, h):
        wait_for(field.at[h, LAYERS], halo_recv.at[0, h])
        last_upper, lower = pitch_face(field, LAYERS - 1, h)
        for f in range(FIELDS):
            lps[h, f] = lower[f]
        halo(1, h, lps.at[h], lpb.at[h], (tm, up, span)).start()

        @pl.when(span == 0)
        def _():
            wait_for(hsb.at[h], halo_recv.at[2, h])

        def body(g, c):
            packed = [zero] * FIELDS
            above = [hsb[h, f, g] for f in range(FIELDS)]
            for j in range(ROWS):
                l = g * ROWS + j
                diff = []
                for f in range(FIELDS):
                    v = field[h, l, f]
                    edge = pltpu.roll(above[f], ROWS - 1 - j, 0) if j < ROWS - 1 else above[f]
                    after = jnp.where(row == ROWS - 1, edge, pltpu.roll(v, ROWS - 1, 0))
                    missing = (row == ROWS - 1) & (span == 1)
                    diff.append(jnp.where(missing, 0.0, 0.5 * (v - after)))
                upper, lower = face(1, l, h, diff)
                for f in range(FIELDS):
                    turned = pltpu.roll(lower[f], 1, 0)
                    acc[h, l, f] += upper[f] + jnp.where(row == 0, 0.0, turned)
                    moved = pltpu.roll(turned, j, 0) if j else turned
                    packed[f] = jnp.where(row == j, moved, packed[f])
            for f in range(FIELDS):
                lss[h, f, g] = packed[f]
            return c
        lax.fori_loop(0, GROUPS, body, 0)

        @pl.when(span == 0)
        def _():
            rows_out(3, h, lss, lsb)

        for f in range(FIELDS):
            acc[h, LAYERS - 1, f] += last_upper[f]

    def couple(h, first):
        def body(f, c):
            out = coupled([inb[h, m, f] for m in range(TIMES)])
            for n in range(TIMES):
                osrc[h, n, f] = out[n]
            return c
        if not first:
            wait_for(osrc.at[h], out_send.at[h])
        lax.fori_loop(0, FIELDS, body, 0)
        for w in targets:
            send_out(h, w)

    def update(field, h, weight, first, last):
        wait_for(lpb.at[h], halo_recv.at[1, h])

        @pl.when(span == 1)
        def _():
            wait_for(lsb.at[h], halo_recv.at[3, h])

        wait_for(outb.at[h], out_recv.at[h])
        sent_field(field, h)
        wait_for(lps.at[h], halo_send.at[1, h])

        @pl.when(span == 0)
        def _():
            wait_for(lss.at[h], halo_send.at[3, h])

        for g in range(GROUPS):
            below = [lsb[h, f, g] for f in range(FIELDS)]
            packed = [None] * FIELDS
            for j in range(ROWS):
                l = g * ROWS + j
                pace = ps[l, :, cols(h)] * np.float32(weight)
                for f in range(FIELDS):
                    moved = pltpu.roll(below[f], ROWS - j, 0) if j else below[f]
                    residual = acc[h, l, f] + outb[h, l, f] + jnp.where(row == 0, moved, 0.0)
                    if l == 0:
                        residual = residual + lpb[h, f]
                    if first:
                        res_ref[0, f, l, :, cols(h)] = residual
                    new = adj[h, l, f] - pace * residual
                    acc[h, l, f] = zero
                    if last:
                        next_ref[0, f, l, :, cols(h)] = new
                    else:
                        cur[h, l, f] = new
                        packed[f] = jnp.where(row == j, pltpu.roll(new, j, 0), packed[f]) if j else new
            if not last:
                for f in range(FIELDS):
                    hss[h, f, g] = packed[f]
        if not last:
            send_field(cur, h)

    field = adj
    for step, weight in enumerate(WEIGHTS):
        first, last = step == 0, step == len(WEIGHTS) - 1
        for what in FIRST if first else ORDER:
            h = int(what[1:] or 0)
            if what[0] == "S":
                send_field(adj, h)
            elif what[0] == "P":
                send_field(adj, h, 0, EARLY)
            elif what[0] == "Q":
                send_field(adj, h, EARLY, TIMES)
            elif what[0] == "L":
                for copy in loads:
                    copy.wait()
            elif what[0] == "F":
                far(field, h)
            elif what[0] == "N":
                near(field)
            elif what[0] == "C":
                wait_for(inb.at[h], in_recv.at[h])
                couple(h, first)
            else:
                update(field, h, weight, first, last)
        field = cur
    for h in range(HALVES):
        wait_for(osrc.at[h], out_send.at[h])


def local(adjoint, source, face_jacobian, dissipation, cell_jacobian, pseudo_step):
    f32 = jnp.float32
    tile = (ROWS, LANES)
    block = (HALVES, LAYERS, FIELDS) + tile
    tall = (HALVES, LAYERS + 1, FIELDS) + tile
    edge = (HALVES, FIELDS) + tile
    rows = (HALVES, FIELDS, GROUPS) + tile
    vmem = [
        tall, tall, block, block, block, block,
        face_jacobian.shape[1:], cell_jacobian.shape[1:], dissipation.shape[1:],
        pseudo_step.shape[1:], source.shape[1:],
        edge, edge, rows, rows, rows, rows,
    ]
    dma = pltpu.SemaphoreType.DMA
    out = jax.ShapeDtypeStruct(adjoint.shape, f32)
    return pl.pallas_call(
        kernel,
        out_shape=(out, out),
        in_specs=[pl.BlockSpec(memory_space=pl.ANY)] * 6,
        out_specs=(pl.BlockSpec(memory_space=pltpu.VMEM),) * 2,
        scratch_shapes=[pltpu.VMEM(s, f32) for s in vmem]
        + [dma((6,)), dma((2,)), dma((2,)), dma((2,)), dma((2,)), dma((4, 2)), dma((4, 2))],
        compiler_params=pltpu.CompilerParams(
            collective_id=0, has_side_effects=True, vmem_limit_bytes=48 * 2**20
        ),
        name="adjoint_update",
    )(*(
        pltpu.with_memory_space_constraint(x, pltpu.HBM)
        for x in (adjoint, source, face_jacobian, dissipation, cell_jacobian, pseudo_step)
    ))


def solution(mesh):
    in_specs = (
        P("tm", None, "pitch", "span", None),
        P("tm", None, "pitch", "span", None),
        P("tm", None, None, None, "pitch", "span", None),
        P("tm", None, "pitch", "span", None),
        P("tm", None, None, "pitch", "span", None),
        P("tm", "pitch", "span", None),
    )
    out_specs = (P("tm", None, "pitch", "span", None), P("tm", None, "pitch", "span", None))
    return jax.shard_map(local, mesh=mesh, in_specs=in_specs, out_specs=out_specs, check_vma=False)
```

```python
import functools
import math

import jax
import jax.numpy as jnp
import numpy as np
from jax import lax
from jax.experimental import pallas as pl
from jax.experimental.pallas import tpu as pltpu
from jax.sharding import PartitionSpec as P

MESH = pl.DeviceIdType.MESH
FREQUENCY = 0.5
VISCOSITY = 0.2
WEIGHTS = (0.6, 0.6, 1.0)
FIELDS, TIMES, LAYERS, ROWS, LANES, HALVES = 5, 16, 16, 8, 128, 2
GROUPS = LAYERS // ROWS
EARLY = 8
FIRST = ("S0", "P1", "L", "Q1", "F0", "C0", "N", "F1", "C1", "U0", "U1")
ORDER = ("F0", "C0", "N", "F1", "C1", "U0", "U1")


def spectral_table():
    k = (np.arange(TIMES)[:, None] - np.arange(TIMES)[None, :]) % TIMES
    angle = np.pi * np.where(k == 0, 1, k) / TIMES
    off = 0.5 * (-1.0) ** k * (FREQUENCY * np.cos(angle) / np.sin(angle) + VISCOSITY / np.sin(angle) ** 2)
    return np.where(k == 0, VISCOSITY * (TIMES * TIMES / 12.0 + 1.0 / 6.0), off)


def coupled(values):
    table = spectral_table()
    half = TIMES // 2
    even = 0.5 * (table[:half, :half] + table[half:, :half])
    odd = 0.5 * (table[:half, :half] - table[half:, :half])
    sums = [values[m] + values[m + half] for m in range(half)]
    diffs = [values[m] - values[m + half] for m in range(half)]
    low, high = [], []
    for n in range(half):
        e = sums[0] * np.float32(even[0, n])
        o = diffs[0] * np.float32(odd[0, n])
        for m in range(1, half):
            e = e + sums[m] * np.float32(even[m, n])
            o = o + diffs[m] * np.float32(odd[m, n])
        low.append(e + o)
        high.append(e - o)
    return low + high


def kernel(
    adj_hbm, src_hbm, fj_hbm, ds_hbm, cj_hbm, ps_hbm,
    next_ref, res_ref,
    adj, cur, acc, inb, osrc, outb, fj, cj, ds, ps, src,
    lps, lpb, hss, hsb, lss, lsb,
    load_sem, in_send, in_recv, out_send, out_recv, halo_send, halo_recv,
):
    tm, pitch, span = lax.axis_index("tm"), lax.axis_index("pitch"), lax.axis_index("span")
    pitches = lax.axis_size("pitch")
    other = 1 - span
    up, down = lax.rem(pitch + 1, pitches), lax.rem(pitch + pitches - 1, pitches)
    zh, y, core = tm // 8, lax.rem(tm // 2, 4), lax.rem(tm, 2)

    def target(k):
        q, j = k // 4, k % 4
        dz, dy, dc = (j // 2 + q // 2) % 2, (2 + 3 * j) % 4, q % 2
        return (lax.rem(zh + dz, 2) * 4 + lax.rem(y + dy, 4)) * 2 + lax.rem(core + dc, 2)

    targets = [target(k) for k in range(TIMES)]
    row = lax.broadcasted_iota(jnp.int32, (ROWS, LANES), 0)
    lane = lax.broadcasted_iota(jnp.int32, (ROWS, LANES), 1)

    def cols(h):
        return slice(h * LANES, (h + 1) * LANES)

    def wait_for(ref, sem):
        pltpu.make_async_copy(ref, ref, sem).wait()

    zero = jnp.zeros((ROWS, LANES), jnp.float32)
    for h in range(HALVES):
        for f in range(FIELDS):
            for g in range(GROUPS):
                hsb[h, f, g] = zero
                lsb[h, f, g] = zero

    barrier = pltpu.get_barrier_semaphore()
    for w in targets:
        pl.semaphore_signal(barrier, inc=1, device_id=(w, pitch, other), device_id_type=MESH)
    for p in (down, up):
        pl.semaphore_signal(barrier, inc=1, device_id=(tm, p, span), device_id_type=MESH)

    for h in range(HALVES):
        for f in range(FIELDS):
            pltpu.make_async_copy(
                adj_hbm.at[0, f, :, :, cols(h)], adj.at[h, pl.ds(0, LAYERS), f], load_sem.at[0]
            ).start()
    loads = [
        pltpu.make_async_copy(a.at[0], b, load_sem.at[1 + i])
        for i, (a, b) in enumerate(
            ((src_hbm, src), (cj_hbm, cj), (fj_hbm, fj), (ds_hbm, ds), (ps_hbm, ps))
        )
    ]
    def pack_first_rows(field, h):
        for f in range(FIELDS):
            for g in range(GROUPS):
                tile = field[h, g * ROWS, f]
                for j in range(1, ROWS):
                    tile = jnp.where(row == j, pltpu.roll(field[h, g * ROWS + j, f], j, 0), tile)
                hss[h, f, g] = tile

    wait_for(adj.at[:, pl.ds(0, LAYERS)], load_sem.at[0])
    for copy in loads:
        copy.start()
    for h in range(HALVES):
        pack_first_rows(adj, h)

    def clear(l, c):
        for h in range(HALVES):
            for f in range(FIELDS):
                acc[h, l, f] = zero
        return c
    lax.fori_loop(0, LAYERS, clear, 0)
    pl.semaphore_wait(barrier, TIMES + 2)

    def send_in(field, h, w):
        pltpu.make_async_remote_copy(
            src_ref=field.at[h, w], dst_ref=inb.at[h, tm],
            send_sem=in_send.at[h], recv_sem=in_recv.at[h],
            device_id=(w, pitch, other), device_id_type=MESH,
        ).start()

    def send_out(h, w):
        pltpu.make_async_remote_copy(
            src_ref=osrc.at[h, w], dst_ref=outb.at[h, tm],
            send_sem=out_send.at[h], recv_sem=out_recv.at[h],
            device_id=(w, pitch, other), device_id_type=MESH,
        ).start()

    def halo(i, h, source, dest, device):
        return pltpu.make_async_remote_copy(
            src_ref=source, dst_ref=dest, send_sem=halo_send.at[i, h], recv_sem=halo_recv.at[i, h],
            device_id=device, device_id_type=MESH,
        )

    def rows_out(i, h, source, dest):
        halo(i, h, source.at[h], dest.at[h], (tm, pitch, other)).start()

    def send_field(field, h, start=0, stop=TIMES):
        if start == 0:
            @pl.when(span == 1)
            def _():
                rows_out(2, h, hss, hsb)

            halo(0, h, field.at[h, 0], field.at[h, LAYERS], (tm, down, span)).start()
        for w in targets[start:stop]:
            send_in(field, h, w)

    def sent_field(field, h):
        @pl.when(span == 1)
        def _():
            wait_for(hss.at[h], halo_send.at[2, h])

        wait_for(field.at[h, 0], halo_send.at[0, h])
        wait_for(field.at[h, pl.ds(0, LAYERS)], in_send.at[h])

    def face(d, l, h, diff):
        turned = []
        for a in range(FIELDS):
            s = fj[d, 0, a, l, :, cols(h)] * diff[0]
            for b in range(1, FIELDS):
                s = s + fj[d, b, a, l, :, cols(h)] * diff[b]
            turned.append(s)
        spread = [ds[d, l, :, cols(h)] * x for x in diff]
        return [t + s for t, s in zip(turned, spread)], [t - s for t, s in zip(turned, spread)]

    def pitch_face(field, l, h):
        diff = [0.5 * (field[h, l, f] - field[h, l + 1, f]) for f in range(FIELDS)]
        return face(0, l, h, diff)

    def near(field):
        def body(l, c, with_pitch):
            carried = None
            for h in range(HALVES):
                v = [field[h, l, f] for f in range(FIELDS)]
                diff = []
                for f in range(FIELDS):
                    after = pltpu.roll(v[f], LANES - 1, 1)
                    if h + 1 < HALVES:
                        beyond = pltpu.roll(field[h + 1, l, f], LANES - 1, 1)
                        diff.append(0.5 * (v[f] - jnp.where(lane == LANES - 1, beyond, after)))
                    else:
                        diff.append(jnp.where(lane == LANES - 1, 0.0, 0.5 * (v[f] - after)))
                upper, lower = face(2, l, h, diff)
                turned = [pltpu.roll(x, 1, 1) for x in lower]
                for f in range(FIELDS):
                    first = 0.0 if carried is None else carried[f]
                    total = acc[h, l, f] - src[f, l, :, cols(h)] + upper[f]
                    for b in range(FIELDS):
                        total = total + cj[b, f, l, :, cols(h)] * v[b]
                    acc[h, l, f] = total + jnp.where(lane == 0, first, turned[f])
                carried = turned
                if with_pitch:
                    upper, lower = pitch_face(field, l, h)
                    for f in range(FIELDS):
                        acc[h, l, f] += upper[f]
                        acc[h, l + 1, f] += lower[f]
            return c
        def group(g, c):
            for j in range(4):
                body(g * 4 + j, 0, with_pitch=True)
            return c
        lax.fori_loop(0, LAYERS // 4 - 1, group, 0)
        for l in range(LAYERS - 4, LAYERS):
            body(l, 0, with_pitch=l < LAYERS - 1)

    def far(field, h):
        wait_for(field.at[h, LAYERS], halo_recv.at[0, h])
        last_upper, lower = pitch_face(field, LAYERS - 1, h)
        for f in range(FIELDS):
            lps[h, f] = lower[f]
        halo(1, h, lps.at[h], lpb.at[h], (tm, up, span)).start()

        @pl.when(span == 0)
        def _():
            wait_for(hsb.at[h], halo_recv.at[2, h])

        def body(g, c):
            packed = [zero] * FIELDS
            above = [hsb[h, f, g] for f in range(FIELDS)]
            for j in range(ROWS):
                l = g * ROWS + j
                diff = []
                for f in range(FIELDS):
                    v = field[h, l, f]
                    edge = pltpu.roll(above[f], ROWS - 1 - j, 0) if j < ROWS - 1 else above[f]
                    after = jnp.where(row == ROWS - 1, edge, pltpu.roll(v, ROWS - 1, 0))
                    missing = (row == ROWS - 1) & (span == 1)
                    diff.append(jnp.where(missing, 0.0, 0.5 * (v - after)))
                upper, lower = face(1, l, h, diff)
                for f in range(FIELDS):
                    turned = pltpu.roll(lower[f], 1, 0)
                    acc[h, l, f] += upper[f] + jnp.where(row == 0, 0.0, turned)
                    moved = pltpu.roll(turned, j, 0) if j else turned
                    packed[f] = jnp.where(row == j, moved, packed[f])
            for f in range(FIELDS):
                lss[h, f, g] = packed[f]
            return c
        lax.fori_loop(0, GROUPS, body, 0)

        @pl.when(span == 0)
        def _():
            rows_out(3, h, lss, lsb)

        for f in range(FIELDS):
            acc[h, LAYERS - 1, f] += last_upper[f]

    def couple(h, first):
        def body(f, c):
            out = coupled([inb[h, m, f] for m in range(TIMES)])
            for n in range(TIMES):
                osrc[h, n, f] = out[n]
            return c
        if not first:
            wait_for(osrc.at[h], out_send.at[h])
        lax.fori_loop(0, FIELDS, body, 0)
        for w in targets:
            send_out(h, w)

    def update(field, h, weight, first, last):
        wait_for(lpb.at[h], halo_recv.at[1, h])

        @pl.when(span == 1)
        def _():
            wait_for(lsb.at[h], halo_recv.at[3, h])

        wait_for(outb.at[h], out_recv.at[h])
        sent_field(field, h)
        wait_for(lps.at[h], halo_send.at[1, h])

        @pl.when(span == 0)
        def _():
            wait_for(lss.at[h], halo_send.at[3, h])

        for g in range(GROUPS):
            below = [lsb[h, f, g] for f in range(FIELDS)]
            packed = [None] * FIELDS
            for j in range(ROWS):
                l = g * ROWS + j
                pace = ps[l, :, cols(h)] * np.float32(weight)
                for f in range(FIELDS):
                    moved = pltpu.roll(below[f], ROWS - j, 0) if j else below[f]
                    residual = acc[h, l, f] + outb[h, l, f] + jnp.where(row == 0, moved, 0.0)
                    if l == 0:
                        residual = residual + lpb[h, f]
                    if first:
                        res_ref[0, f, l, :, cols(h)] = residual
                    new = adj[h, l, f] - pace * residual
                    if last:
                        next_ref[0, f, l, :, cols(h)] = new
                    else:
                        acc[h, l, f] = zero
                        cur[h, l, f] = new
                        packed[f] = jnp.where(row == j, pltpu.roll(new, j, 0), packed[f]) if j else new
            if not last:
                for f in range(FIELDS):
                    hss[h, f, g] = packed[f]
        if not last:
            send_field(cur, h)

    field = adj
    for step, weight in enumerate(WEIGHTS):
        first, last = step == 0, step == len(WEIGHTS) - 1
        for what in FIRST if first else ORDER:
            h = int(what[1:] or 0)
            if what[0] == "S":
                send_field(adj, h)
            elif what[0] == "P":
                send_field(adj, h, 0, EARLY)
            elif what[0] == "Q":
                send_field(adj, h, EARLY, TIMES)
            elif what[0] == "L":
                for copy in loads:
                    copy.wait()
            elif what[0] == "F":
                far(field, h)
            elif what[0] == "N":
                near(field)
            elif what[0] == "C":
                wait_for(inb.at[h], in_recv.at[h])
                couple(h, first)
            else:
                update(field, h, weight, first, last)
        field = cur
    for h in range(HALVES):
        wait_for(osrc.at[h], out_send.at[h])


def local(adjoint, source, face_jacobian, dissipation, cell_jacobian, pseudo_step):
    f32 = jnp.float32
    tile = (ROWS, LANES)
    block = (HALVES, LAYERS, FIELDS) + tile
    tall = (HALVES, LAYERS + 1, FIELDS) + tile
    edge = (HALVES, FIELDS) + tile
    rows = (HALVES, FIELDS, GROUPS) + tile
    vmem = [
        tall, tall, block, block, block, block,
        face_jacobian.shape[1:], cell_jacobian.shape[1:], dissipation.shape[1:],
        pseudo_step.shape[1:], source.shape[1:],
        edge, edge, rows, rows, rows, rows,
    ]
    dma = pltpu.SemaphoreType.DMA
    out = jax.ShapeDtypeStruct(adjoint.shape, f32)
    return pl.pallas_call(
        kernel,
        out_shape=(out, out),
        in_specs=[pl.BlockSpec(memory_space=pl.ANY)] * 6,
        out_specs=(pl.BlockSpec(memory_space=pltpu.VMEM),) * 2,
        scratch_shapes=[pltpu.VMEM(s, f32) for s in vmem]
        + [dma((6,)), dma((2,)), dma((2,)), dma((2,)), dma((2,)), dma((4, 2)), dma((4, 2))],
        compiler_params=pltpu.CompilerParams(
            collective_id=0, has_side_effects=True, vmem_limit_bytes=48 * 2**20
        ),
        name="adjoint_update",
    )(*(
        pltpu.with_memory_space_constraint(x, pltpu.HBM)
        for x in (adjoint, source, face_jacobian, dissipation, cell_jacobian, pseudo_step)
    ))


def solution(mesh):
    in_specs = (
        P("tm", None, "pitch", "span", None),
        P("tm", None, "pitch", "span", None),
        P("tm", None, None, None, "pitch", "span", None),
        P("tm", None, "pitch", "span", None),
        P("tm", None, None, "pitch", "span", None),
        P("tm", "pitch", "span", None),
    )
    out_specs = (P("tm", None, "pitch", "span", None), P("tm", None, "pitch", "span", None))
    return jax.shard_map(local, mesh=mesh, in_specs=in_specs, out_specs=out_specs, check_vma=False)
```
